32 devices in a mesh: rep: 2 (over y), chol: 8 (over z, x), pop: 2 (over core).
Axes of the slice: x: 2, y: 2, z: 4, core: 2. Of those that a mesh axis runs over, the one named last changes fastest.
Arguments:
- green_half: bfloat16 [256, 16, 1024], P(('rep', 'chol'), 'pop'), parts along dimension 0, may hold values from -5 to 5
- step_delta: bfloat16 [256, 16, 1024], P(('rep', 'chol'), 'pop'), parts along dimension 0, may hold values from -4 to 4
- chol_vectors: bfloat16 [96, 128, 1024], P(('rep', 'chol')), parts along dimension 0, as said below
- copy_counts: int32 [32], P(('rep', 'pop')), parts along dimension 0, may hold values from 0 to 2, as said below
- parents: int32 [32], P('rep'), parts along dimension 0, may hold values from 0 to 15, as said below
Outputs:
- parent_force: bfloat16 [256, 16, 1024], P(('rep', 'chol'), 'pop'), parts along dimension 0
- child_energy: float32 [32], P(('rep', 'pop')), parts along dimension 0
The draws below stay inside these ranges and needn't reach their ends.
There are 2 independent parts, one for each index of `rep`. The reference program is written for one: setup_inputs(seed, part) draws one part's arguments, and reference() takes and returns one part's arrays. A program takes and returns all parts, laid end to end along the dimension named above; each array names one. Nothing has to cross between parts.
Inputs may be any that keep to these rules, and one draw needn't show every extreme that they name: copy_counts[p] is the number of children c with parents[c] = p; the counts sum to 16; some walker has 0 copies and some has 2. parents never falls from one child to the next; the first child's parent is walker 0 and the last child's is walker 16 - 1; each child's parent is the child itself or a walker next to it. `chol_vectors`: entries are of order 1 / sqrt(1024) times a factor per vector.
All inputs are finite; a program needn't handle non-finite values.
Results may differ from the reference program's by a relative error of at most 0.0057.
Values may be sent and summed in bfloat16 or wider, within the bound.
A program may use at most 64 MiB of HBM per device.

```python
import math
import jax
import jax.numpy as jnp
from jax import lax

NOCC = 128
NBASIS = 1024
CHOL_DEV = 6
NCHOL = 48
WALKERS = 16
N_CHOL = 8


def draw_green_half(key, part):
    folded = jax.random.fold_in(key, 11)
    key_values, key_rows, key_columns = jax.random.split(folded, 3)
    dims_all = (NOCC, WALKERS, NBASIS)
    values = jax.random.truncated_normal(key_values, -4.0, 4.0, dims_all, jnp.float32)
    row_lower = 0.03
    row_upper = 0.3
    column_lower = 0.3
    column_upper = 3.0
    row_scale = jnp.exp(jax.random.uniform(key_rows, (NOCC, WALKERS, 1), jnp.float32, math.log(row_lower), math.log(row_upper)))
    column_scale = jnp.exp(jax.random.uniform(key_columns, (1, WALKERS, NBASIS), jnp.float32, math.log(column_lower), math.log(column_upper)))
    return (values * row_scale * column_scale).astype(jnp.bfloat16)


def draw_chol_vectors(key, part):
    folded = jax.random.fold_in(key, 23)
    key_values, key_rough = jax.random.split(folded)
    dims_all = (NCHOL, NOCC, NBASIS)
    position = jnp.arange(NCHOL, dtype=jnp.float32) / (NCHOL - 1)
    rough = jnp.exp(jax.random.uniform(key_rough, (NCHOL,), jnp.float32, math.log(0.7), math.log(1.4)))
    ramp = jnp.exp(position * math.log(3.0)) * rough
    values = jax.random.truncated_normal(key_values, -4.0, 4.0, dims_all, jnp.float32)
    return (values * ramp[:, None, None] / NBASIS ** 0.5).astype(jnp.bfloat16)


def resample(key):
    folded = jax.random.fold_in(key, 5)
    key_offset, key_picks, key_which, key_forced = jax.random.split(folded, 4)
    half_count = WALKERS // 2
    offset = jax.random.randint(key_offset, (), 0, 2, dtype=jnp.int32)
    pairs_live = ((WALKERS - offset) // 2).astype(jnp.int32)
    picks = jax.random.randint(key_picks, (half_count,), 0, 3, dtype=jnp.int32)
    chosen = jax.random.randint(key_which, (), 0, pairs_live, dtype=jnp.int32)
    forced = jax.random.randint(key_forced, (), 1, 3, dtype=jnp.int32)
    pair_index = jnp.arange(half_count, dtype=jnp.int32)
    picks = jnp.where(pair_index == chosen, forced, picks).astype(jnp.int32)
    pair_first = (offset + 2 * pair_index).astype(jnp.int32)
    picks = jnp.where((pair_first == 0) & (picks == 2), 1, picks).astype(jnp.int32)
    picks = jnp.where((pair_first + 1 == WALKERS - 1) & (picks == 1), 2, picks).astype(jnp.int32)
    walker_ids = jnp.arange(WALKERS, dtype=jnp.int32)
    shifted = (walker_ids - offset).astype(jnp.int32)
    pair_ids = jnp.floor_divide(shifted, 2).astype(jnp.int32)
    live = (shifted >= 0) & (pair_ids < pairs_live)
    safe_ids = jnp.clip(pair_ids, 0, half_count - 1).astype(jnp.int32)
    pair_pick = jnp.take(picks, safe_ids)
    start_of = (offset + 2 * safe_ids).astype(jnp.int32)
    parent_ids = jnp.where(pair_pick == 1, start_of, jnp.where(pair_pick == 2, start_of + 1, walker_ids))
    parent_ids = jnp.where(live, parent_ids, walker_ids).astype(jnp.int32)
    counts = jnp.sum((parent_ids[:, None] == walker_ids[None, :]).astype(jnp.int32), axis=0)
    return (counts.astype(jnp.int32), parent_ids)


def draw_copy_counts(key, part):
    return resample(key)[0]


def draw_parents(key, part):
    return resample(key)[1]


def shard_levels(key, dims, shards, low, largest):
    gain = 1.0
    for dim, blocks in shards:
        draws = jax.random.uniform(jax.random.fold_in(jax.random.fold_in(key, 6), dim), (blocks,), jnp.float32, low / len(shards), largest / len(shards))
        gain = gain * jnp.repeat(jnp.exp(draws), dims[dim] // blocks).reshape((-1,) + (1,) * (len(dims) - 1 - dim))
    return gain


def gaussian(rng, shape, width, most, shards=(), kind=jnp.bfloat16):
    array = jax.random.normal(rng, shape, jnp.float32) * width
    if len(shards) > 0:
        array = shard_levels(rng, shape, shards, -0.22, 0.18) * array
    return jnp.clip(array, min=-most, max=most).astype(kind)


def setup_inputs(seed: int = 0, part: int = 0) -> dict:
    splits = jax.random.split(jax.random.key(seed), 6)
    part_splits = jax.random.split(jax.random.fold_in(splits[5], part), 6)
    green_half = draw_green_half(jax.random.fold_in(jax.random.fold_in(splits[5], part), 71), part)
    step_delta = gaussian(part_splits[1], (NOCC, WALKERS, NBASIS), 0.5, 4.0, ((0, 8), (1, 2)))
    chol_vectors = draw_chol_vectors(jax.random.fold_in(jax.random.fold_in(splits[5], part), 71), part)
    copy_counts = draw_copy_counts(jax.random.fold_in(jax.random.fold_in(splits[5], part), 71), part)
    parents = draw_parents(jax.random.fold_in(jax.random.fold_in(splits[5], part), 71), part)
    return {"green_half": green_half, "step_delta": step_delta, "chol_vectors": chol_vectors, "copy_counts": copy_counts, "parents": parents}


def reference(green_half, step_delta, chol_vectors, copy_counts, parents):
    picked = jnp.take(green_half, parents, axis=1).astype(jnp.float32)
    child_rows = (picked + step_delta.astype(jnp.float32)).astype(jnp.bfloat16)
    child_wide = child_rows.astype(jnp.float32)
    factor = -1.0 / (NCHOL ** 0.5)
    chol_blocks = chol_vectors.reshape(N_CHOL, CHOL_DEV, NOCC, NBASIS)

    def accumulate(state_pair, chol_block):
        force_sum, traces = state_pair
        vectors = chol_block.astype(jnp.float32)
        cross = jnp.einsum("iwm,gkm->wgik", child_wide, vectors, precision=lax.Precision.HIGHEST)
        cross_low = lax.optimization_barrier(cross.astype(jnp.bfloat16)).astype(jnp.float32)
        force_sum = force_sum + factor * jnp.einsum("wgik,gil->kwl", cross_low, vectors, precision=lax.Precision.HIGHEST)
        traces = traces + jnp.sum(cross_low * jnp.swapaxes(cross, 2, 3), axis=(1, 2, 3))
        return (force_sum, traces), None

    start_state = (jnp.zeros((NOCC, WALKERS, NBASIS), jnp.float32), jnp.zeros((WALKERS,), jnp.float32))
    final_state, unused = lax.scan(accumulate, start_state, chol_blocks)
    force_sum, traces = final_state
    child_energy = (-0.125 / (NCHOL * NOCC)) * traces
    one_hot = (parents[:, None] == jnp.arange(WALKERS, dtype=jnp.int32)[None, :]).astype(jnp.float32)
    summed = jnp.einsum("kcl,cp->kpl", force_sum, one_hot, precision=lax.Precision.HIGHEST)
    divisor = jnp.maximum(copy_counts, 1).astype(jnp.float32)
    return (summed / divisor[None, :, None]).astype(jnp.bfloat16), child_energy
```

```python
import functools

import jax
import jax.numpy as jnp
from jax import lax
from jax.experimental import pallas as pl
from jax.experimental.pallas import tpu as pltpu
from jax.sharding import PartitionSpec as P

MESH = pl.DeviceIdType.MESH
CHUNK = 2


def child_forces(child_rows, chol_vectors):
    total_chol = lax.axis_size("chol") * chol_vectors.shape[0]
    orbitals = chol_vectors.shape[1]
    factor = -1.0 / total_chol**0.5
    cross = jnp.einsum(
        "iwm,gkm->wgik",
        lax.all_gather(child_rows, "chol", axis=0, tiled=True),
        chol_vectors,
        preferred_element_type=jnp.float32,
    )
    cross_low = cross.astype(jnp.bfloat16)
    trace_part = jnp.sum(cross_low.astype(jnp.float32) * jnp.swapaxes(cross, 2, 3), axis=(1, 2, 3))
    energies = lax.psum(trace_part, "chol") * (-0.125 / (total_chol * orbitals))
    forces = lax.psum_scatter(
        factor
        * jnp.einsum("wgik,gil->kwl", cross_low, chol_vectors, preferred_element_type=jnp.float32),
        "chol",
        scatter_dimension=0,
        tiled=True,
    )
    return (forces, energies)


def shards(green_half, step_delta, chol_vectors, copy_counts, parents):
    per_group = green_half.shape[1]
    my_group = lax.axis_index("pop")
    all_parents = lax.all_gather(green_half, "pop", axis=1, tiled=True)
    my_parents = lax.dynamic_slice_in_dim(parents, my_group * per_group, per_group, 0)
    picked = jnp.take(all_parents, my_parents, axis=1)
    child_rows = (picked.astype(jnp.float32) + step_delta.astype(jnp.float32)).astype(jnp.bfloat16)
    forces, child_energy = child_forces(child_rows, chol_vectors)
    parent_slots = jnp.arange(all_parents.shape[1], dtype=jnp.int32)
    one_hot = (my_parents[:, None] == parent_slots[None, :]).astype(jnp.float32)
    spread_sum = jnp.einsum("kcl,cp->kpl", forces, one_hot, precision=lax.Precision.HIGHEST)
    summed = lax.psum_scatter(
        spread_sum.astype(jnp.bfloat16), "pop", scatter_dimension=1, tiled=True
    ).astype(jnp.float32)
    divisor = jnp.maximum(copy_counts, 1).astype(jnp.float32)
    parent_force = (summed / divisor[None, :, None]).astype(jnp.bfloat16)
    return (parent_force, child_energy)


def ring_device(pos, n):
    half = n // 2
    pos = lax.rem(pos + 2 * n, n)
    side = lax.div(pos, half)
    rest = lax.rem(pos, half)
    return 2 * ((1 - side) * rest + side * (half - 1 - rest)) + side


def step_kernel(
    n, parents, counts, green, delta, chol, out, energy_out,
    gpad, gall, cross, force, fsend, arrived, final, edge, traces,
    ag_send, ag_recv, rs_send, rs_recv, tr_send, tr_recv, edge_send, edge_recv,
):
    walkers, rows, basis = green.shape
    vectors, orbitals, _ = chol.shape
    chunks = walkers // CHUNK
    me = lax.axis_index("chol")
    pop = lax.axis_index("pop")
    side = lax.rem(me, 2)
    level = lax.div(me, 2)
    pos = side * (n - 1 - level) + (1 - side) * level
    hops = (n // 2, n - 1 - n // 2)
    scale = -1.0 / (n * vectors) ** 0.5

    def first_walker(ch):
        late = jnp.minimum(lax.div(ch, 2), 1)
        k = late * ch + (1 - late) * (1 - ch)
        return CHUNK * (pop * k + (1 - pop) * (chunks - 1 - k))

    def sign(ch, chain):
        up = 1 - 2 * lax.rem(ch, 2)
        return up if chain == 0 else -up

    def orbital_rows(device):
        return pl.ds(pl.multiple_of(device * rows, rows), rows)

    def gather(ch, chain, step):
        way = sign(ch, chain)
        where = (pl.ds(first_walker(ch), CHUNK), orbital_rows(ring_device(pos - way * step, n)))
        return pltpu.make_async_remote_copy(
            src_ref=gall.at[where],
            dst_ref=gall.at[where],
            send_sem=ag_send.at[chain, step, ch],
            recv_sem=ag_recv.at[chain, step, ch],
            device_id={"chol": ring_device(pos + way, n)},
            device_id_type=MESH,
        )

    def gather_arrival(ch, chain, step):
        way = sign(ch, chain)
        where = (pl.ds(first_walker(ch), CHUNK), orbital_rows(ring_device(pos - way * (step + 1), n)))
        return pltpu.make_async_remote_copy(
            src_ref=gall.at[where],
            dst_ref=gall.at[where],
            send_sem=ag_send.at[chain, step, ch],
            recv_sem=ag_recv.at[chain, step, ch],
            device_id={"chol": ring_device(pos + way, n)},
            device_id_type=MESH,
        )

    def scatter(ch, chain, step):
        way = sign(ch, chain)
        target = orbital_rows(ring_device(pos + way * (hops[chain] - step), n))
        return pltpu.make_async_remote_copy(
            src_ref=fsend.at[pl.ds(first_walker(ch), CHUNK), target],
            dst_ref=arrived.at[chain, step, ch],
            send_sem=rs_send.at[chain, step, ch],
            recv_sem=rs_recv.at[chain, step, ch],
            device_id={"chol": ring_device(pos + way, n)},
            device_id_type=MESH,
        )

    def start_scatter(ch, chain, step):
        way = sign(ch, chain)
        target = orbital_rows(ring_device(pos + way * (hops[chain] - step), n))
        w0 = first_walker(ch)
        for j in range(CHUNK):
            part = force[w0 + j, target, :]
            if step > 0:
                part = part + arrived[chain, step - 1, ch, j].astype(jnp.float32)
            fsend[w0 + j, target, :] = part.astype(jnp.bfloat16)
        scatter(ch, chain, step).start()

    def trace_copy(offset, owner, peer):
        return pltpu.make_async_remote_copy(
            src_ref=traces.at[owner],
            dst_ref=traces.at[owner],
            send_sem=tr_send.at[offset],
            recv_sem=tr_recv.at[offset],
            device_id={"chol": peer},
            device_id_type=MESH,
        )

    barrier = pltpu.get_barrier_semaphore()
    for offset in range(1, n):
        pl.semaphore_signal(
            barrier, inc=1, device_id={"chol": lax.rem(me + offset, n)}, device_id_type=MESH
        )
    pl.semaphore_signal(barrier, inc=1, device_id={"pop": 1 - pop}, device_id_type=MESH)
    gpad[pop * (walkers + 1)] = jnp.zeros((rows, basis), jnp.bfloat16)
    gpad[pl.ds(1, walkers)] = green[...]
    pl.semaphore_wait(barrier, n)

    edge_green = pltpu.make_async_remote_copy(
        src_ref=green.at[(1 - pop) * (walkers - 1)],
        dst_ref=gpad.at[pop * (walkers + 1)],
        send_sem=edge_send.at[0],
        recv_sem=edge_recv.at[0],
        device_id={"pop": 1 - pop},
        device_id_type=MESH,
    )
    edge_green_arrival = pltpu.make_async_remote_copy(
        src_ref=green.at[(1 - pop) * (walkers - 1)],
        dst_ref=gpad.at[(1 - pop) * (walkers + 1)],
        send_sem=edge_send.at[0],
        recv_sem=edge_recv.at[0],
        device_id={"pop": 1 - pop},
        device_id_type=MESH,
    )
    edge_green.start()

    for ch in range(chunks):
        if ch == 1:
            edge_green_arrival.wait_recv()
        w0 = first_walker(jnp.int32(ch))
        for j in range(CHUNK):
            child = pop * walkers + w0 + j
            parent = parents[child]
            row = delta[w0 + j].astype(jnp.float32)
            for k in range(3):
                chosen = jnp.where(parent == child - 1 + k, 1.0, 0.0)
                row = row + chosen * gpad[w0 + j + k].astype(jnp.float32)
            gall[w0 + j, orbital_rows(me), :] = row.astype(jnp.bfloat16)
        for chain in range(2):
            gather(jnp.int32(ch), chain, 0).start()

    for step in range(1, hops[0]):

        def forward(ch, carry, step=step):
            for chain in range(2):
                if step < hops[chain]:
                    gather_arrival(ch, chain, step - 1).wait_recv()
                    gather(ch, chain, step).start()
            return carry

        lax.fori_loop(0, chunks, forward, 0)

    row_ids = lax.broadcasted_iota(jnp.int32, (orbitals, 2 * orbitals), 0)
    col_ids = lax.broadcasted_iota(jnp.int32, (orbitals, 2 * orbitals), 1)
    diagonal = (row_ids == col_ids) | (row_ids + orbitals == col_ids)
    walker_ids = lax.broadcasted_iota(jnp.int32, (walkers, orbitals), 0)

    def compute(ch, total):
        for chain in range(2):
            gather_arrival(ch, chain, hops[chain] - 1).wait_recv()
        w0 = first_walker(ch)
        children = gall[pl.ds(w0, CHUNK)].reshape(CHUNK * orbitals, basis)
        turned = lax.dot_general(
            chol[...].reshape(vectors * orbitals, basis),
            children,
            (((1,), (1,)), ((), ())),
            preferred_element_type=jnp.float32,
        )
        low = turned.astype(jnp.bfloat16)
        rest = (turned - low.astype(jnp.float32)).astype(jnp.bfloat16)
        for j in range(CHUNK):
            mine = slice(j * orbitals, (j + 1) * orbitals)
            for g in range(vectors):
                cross[mine, g * orbitals : (g + 1) * orbitals] = low[
                    g * orbitals : (g + 1) * orbitals, mine
                ]
            products = jnp.dot(
                cross[mine, :],
                jnp.concatenate([low[:, mine], rest[:, mine]], axis=1),
                preferred_element_type=jnp.float32,
            )
            line = jnp.sum(jnp.where(diagonal, products, 0.0), axis=0, keepdims=True)
            line = line[:, :orbitals] + line[:, orbitals:]
            total = total + jnp.where(walker_ids == w0 + j, line, 0.0)
        force[pl.ds(w0, CHUNK)] = jnp.dot(
            cross[...],
            chol[...].reshape(vectors * orbitals, basis),
            preferred_element_type=jnp.float32,
        ).reshape(CHUNK, orbitals, basis)
        for chain in range(2):
            start_scatter(ch, chain, 0)
        return total

    traces[me] = lax.fori_loop(0, chunks, compute, jnp.zeros((walkers, orbitals), jnp.float32))
    for offset in range(1, n):
        trace_copy(offset - 1, me, lax.rem(me + offset, n)).start()

    for step in range(1, hops[0]):

        def add_and_forward(ch, carry, step=step):
            for chain in range(2):
                if step < hops[chain]:
                    scatter(ch, chain, step - 1).wait_recv()
                    start_scatter(ch, chain, step)
            return carry

        lax.fori_loop(0, chunks, add_and_forward, 0)

    edge_force = pltpu.make_async_remote_copy(
        src_ref=edge.at[0],
        dst_ref=edge.at[1],
        send_sem=edge_send.at[1],
        recv_sem=edge_recv.at[1],
        device_id={"pop": 1 - pop},
        device_id_type=MESH,
    )
    final[pop * (walkers + 1)] = jnp.zeros((rows, basis), jnp.float32)
    for ch in range(chunks):
        at = jnp.int32(ch)
        w0 = first_walker(at)
        for chain in range(2):
            scatter(at, chain, hops[chain] - 1).wait_recv()
        for j in range(CHUNK):
            final[w0 + j + 1] = scale * (
                force[w0 + j, orbital_rows(me), :]
                + arrived[0, hops[0] - 1, ch, j].astype(jnp.float32)
                + arrived[1, hops[1] - 1, ch, j].astype(jnp.float32)
            )
        if ch == 1:
            edge[0] = final[1 + (1 - pop) * (walkers - 1)].astype(jnp.bfloat16)
            edge_force.start()

    edge_force.wait_recv()
    final[(1 - pop) * (walkers + 1)] = edge[1].astype(jnp.float32)
    for w in range(walkers):
        parent = pop * walkers + w
        row = jnp.zeros((rows, basis), jnp.float32)
        for k in range(3):
            child = parent - 1 + k
            inside = (child >= 0) & (child < 2 * walkers)
            taken = parents[jnp.minimum(jnp.maximum(child, 0), 2 * walkers - 1)] == parent
            row = row + jnp.where(inside & taken, 1.0, 0.0) * final[w + k]
        copies = jnp.maximum(counts[w], 1).astype(jnp.float32)
        out[w] = (row / jnp.full((rows, basis), copies)).astype(jnp.bfloat16)

    for offset in range(1, n):
        trace_copy(offset - 1, lax.rem(me + n - offset, n), me).wait_recv()
    energy = traces[0]
    for i in range(1, n):
        energy = energy + traces[i]
    energy_out[...] = energy

    edge_green.wait_send()
    edge_force.wait_send()
    for offset in range(1, n):
        trace_copy(offset - 1, me, lax.rem(me + offset, n)).wait_send()

    def drain(ch, carry):
        for chain in range(2):
            for step in range(hops[chain]):
                gather(ch, chain, step).wait_send()
                scatter(ch, chain, step).wait_send()
        return carry

    lax.fori_loop(0, chunks, drain, 0)


def ring_shards(green_half, step_delta, chol_vectors, copy_counts, parents):
    n = lax.axis_size("chol")
    rows, walkers, basis = green_half.shape
    vectors, orbitals, _ = chol_vectors.shape
    chunks = walkers // CHUNK
    hops = n // 2
    smem = pl.BlockSpec(memory_space=pltpu.SMEM)
    vmem = pl.BlockSpec(memory_space=pltpu.VMEM)
    dma = pltpu.SemaphoreType.DMA
    wide = vectors * orbitals
    out, traces = pl.pallas_call(
        functools.partial(step_kernel, n),
        out_shape=(
            jax.ShapeDtypeStruct((walkers, rows, basis), jnp.bfloat16),
            jax.ShapeDtypeStruct((walkers, orbitals), jnp.float32),
        ),
        in_specs=[smem, smem, vmem, vmem, vmem],
        out_specs=(vmem, vmem),
        scratch_shapes=[
            pltpu.VMEM((walkers + 2, rows, basis), jnp.bfloat16),
            pltpu.VMEM((walkers, orbitals, basis), jnp.bfloat16),
            pltpu.VMEM((CHUNK * orbitals, wide), jnp.bfloat16),
            pltpu.VMEM((walkers, orbitals, basis), jnp.float32),
            pltpu.VMEM((walkers, orbitals, basis), jnp.bfloat16),
            pltpu.VMEM((2, hops, chunks, CHUNK, rows, basis), jnp.bfloat16),
            pltpu.VMEM((walkers + 2, rows, basis), jnp.float32),
            pltpu.VMEM((2, rows, basis), jnp.bfloat16),
            pltpu.VMEM((n, walkers, orbitals), jnp.float32),
            dma((2, hops, chunks)),
            dma((2, hops, chunks)),
            dma((2, hops, chunks)),
            dma((2, hops, chunks)),
            dma((n - 1,)),
            dma((n - 1,)),
            dma((2,)),
            dma((2,)),
        ],
        compiler_params=pltpu.CompilerParams(
            collective_id=0, has_side_effects=True, vmem_limit_bytes=40 * 1024 * 1024
        ),
        cost_estimate=pl.CostEstimate(
            flops=4 * walkers * orbitals * wide * basis,
            bytes_accessed=4 * walkers * orbitals * basis,
            transcendentals=0,
        ),
    )(
        parents,
        copy_counts,
        jnp.swapaxes(green_half, 0, 1),
        jnp.swapaxes(step_delta, 0, 1),
        chol_vectors,
    )
    energy = jnp.sum(traces, axis=1) * (-0.125 / (n * vectors * orbitals))
    return jnp.swapaxes(out, 0, 1), energy


def any_shards(green_half, step_delta, chol_vectors, copy_counts, parents):
    rows, walkers, basis = green_half.shape
    orbitals = chol_vectors.shape[1]
    n = lax.axis_size("chol")
    fits = (
        rows % 16 == 0
        and orbitals % 128 == 0
        and basis % 128 == 0
        and walkers == 4 * CHUNK
        and n % 2 == 0
        and n >= 4
        and lax.axis_size("pop") == 2
    )
    run = ring_shards if fits else shards
    return run(green_half, step_delta, chol_vectors, copy_counts, parents)


def solution(mesh):
    placed = (
        P(("rep", "chol"), "pop", None),
        P(("rep", "chol"), "pop", None),
        P(("rep", "chol"), None, None),
        P(("rep", "pop")),
        P("rep"),
    )
    return jax.shard_map(
        any_shards,
        mesh=mesh,
        in_specs=placed,
        out_specs=(P(("rep", "chol"), "pop", None), P(("rep", "pop"))),
        check_vma=False,
    )
```

```python
import functools

import jax
import jax.numpy as jnp
from jax import lax
from jax.experimental import pallas as pl
from jax.experimental.pallas import tpu as pltpu
from jax.sharding import PartitionSpec as P

MESH = pl.DeviceIdType.MESH
CHUNK = 2


def child_forces(child_rows, chol_vectors):
    total_chol = lax.axis_size("chol") * chol_vectors.shape[0]
    orbitals = chol_vectors.shape[1]
    factor = -1.0 / total_chol**0.5
    cross = jnp.einsum(
        "iwm,gkm->wgik",
        lax.all_gather(child_rows, "chol", axis=0, tiled=True),
        chol_vectors,
        preferred_element_type=jnp.float32,
    )
    cross_low = cross.astype(jnp.bfloat16)
    trace_part = jnp.sum(cross_low.astype(jnp.float32) * jnp.swapaxes(cross, 2, 3), axis=(1, 2, 3))
    energies = lax.psum(trace_part, "chol") * (-0.125 / (total_chol * orbitals))
    forces = lax.psum_scatter(
        factor
        * jnp.einsum("wgik,gil->kwl", cross_low, chol_vectors, preferred_element_type=jnp.float32),
        "chol",
        scatter_dimension=0,
        tiled=True,
    )
    return (forces, energies)


def shards(green_half, step_delta, chol_vectors, copy_counts, parents):
    per_group = green_half.shape[1]
    my_group = lax.axis_index("pop")
    all_parents = lax.all_gather(green_half, "pop", axis=1, tiled=True)
    my_parents = lax.dynamic_slice_in_dim(parents, my_group * per_group, per_group, 0)
    picked = jnp.take(all_parents, my_parents, axis=1)
    child_rows = (picked.astype(jnp.float32) + step_delta.astype(jnp.float32)).astype(jnp.bfloat16)
    forces, child_energy = child_forces(child_rows, chol_vectors)
    parent_slots = jnp.arange(all_parents.shape[1], dtype=jnp.int32)
    one_hot = (my_parents[:, None] == parent_slots[None, :]).astype(jnp.float32)
    spread_sum = jnp.einsum("kcl,cp->kpl", forces, one_hot, precision=lax.Precision.HIGHEST)
    summed = lax.psum_scatter(
        spread_sum.astype(jnp.bfloat16), "pop", scatter_dimension=1, tiled=True
    ).astype(jnp.float32)
    divisor = jnp.maximum(copy_counts, 1).astype(jnp.float32)
    parent_force = (summed / divisor[None, :, None]).astype(jnp.bfloat16)
    return (parent_force, child_energy)


def ring_device(pos, n):
    half = n // 2
    pos = lax.rem(pos + 2 * n, n)
    side = lax.div(pos, half)
    rest = lax.rem(pos, half)
    return 2 * ((1 - side) * rest + side * (half - 1 - rest)) + side


def step_kernel(
    n, parents, counts, green_in, delta_in, chol_in, out, energy_out,
    green, delta, chol, gpad, dturn, gall, cross, force, fsend, arrived, final, edge, traces,
    ag_send, ag_recv, rs_send, rs_recv, tr_send, tr_recv, edge_send, edge_recv, load_sem,
):
    rows, walkers, basis = green.shape
    vectors, orbitals, _ = chol.shape
    chunks = walkers // CHUNK
    me = lax.axis_index("chol")
    pop = lax.axis_index("pop")
    side = lax.rem(me, 2)
    level = lax.div(me, 2)
    pos = side * (n - 1 - level) + (1 - side) * level
    hops = (n // 2, n - 1 - n // 2)
    scale = -1.0 / (n * vectors) ** 0.5

    def first_walker(ch):
        late = jnp.minimum(lax.div(ch, 2), 1)
        k = late * ch + (1 - late) * (1 - ch)
        return CHUNK * (pop * k + (1 - pop) * (chunks - 1 - k))

    def sign(ch, chain):
        up = 1 - 2 * lax.rem(ch, 2)
        return up if chain == 0 else -up

    def orbital_rows(device):
        return pl.ds(pl.multiple_of(device * rows, rows), rows)

    def gather(ch, chain, step):
        way = sign(ch, chain)
        where = (pl.ds(first_walker(ch), CHUNK), orbital_rows(ring_device(pos - way * step, n)))
        return pltpu.make_async_remote_copy(
            src_ref=gall.at[where],
            dst_ref=gall.at[where],
            send_sem=ag_send.at[chain, step, ch],
            recv_sem=ag_recv.at[chain, step, ch],
            device_id={"chol": ring_device(pos + way, n)},
            device_id_type=MESH,
        )

    def gather_arrival(ch, chain, step):
        way = sign(ch, chain)
        where = (pl.ds(first_walker(ch), CHUNK), orbital_rows(ring_device(pos - way * (step + 1), n)))
        return pltpu.make_async_remote_copy(
            src_ref=gall.at[where],
            dst_ref=gall.at[where],
            send_sem=ag_send.at[chain, step, ch],
            recv_sem=ag_recv.at[chain, step, ch],
            device_id={"chol": ring_device(pos + way, n)},
            device_id_type=MESH,
        )

    def scatter(ch, chain, step):
        way = sign(ch, chain)
        target = orbital_rows(ring_device(pos + way * (hops[chain] - step), n))
        return pltpu.make_async_remote_copy(
            src_ref=fsend.at[pl.ds(first_walker(ch), CHUNK), target],
            dst_ref=arrived.at[chain, step, ch],
            send_sem=rs_send.at[chain, step, ch],
            recv_sem=rs_recv.at[chain, step, ch],
            device_id={"chol": ring_device(pos + way, n)},
            device_id_type=MESH,
        )

    def start_scatter(ch, chain, step):
        way = sign(ch, chain)
        target = orbital_rows(ring_device(pos + way * (hops[chain] - step), n))
        w0 = first_walker(ch)
        for j in range(CHUNK):
            part = force[w0 + j, target, :]
            if step > 0:
                part = part + arrived[chain, step - 1, ch, j].astype(jnp.float32)
            fsend[w0 + j, target, :] = part.astype(jnp.bfloat16)
        scatter(ch, chain, step).start()

    def trace_copy(offset, owner, peer):
        return pltpu.make_async_remote_copy(
            src_ref=traces.at[owner],
            dst_ref=traces.at[owner],
            send_sem=tr_send.at[offset],
            recv_sem=tr_recv.at[offset],
            device_id={"chol": peer},
            device_id_type=MESH,
        )

    loads = [
        pltpu.make_async_copy(green_in, green, load_sem.at[0]),
        pltpu.make_async_copy(delta_in, delta, load_sem.at[1]),
        pltpu.make_async_copy(chol_in, chol, load_sem.at[2]),
    ]
    for load in loads:
        load.start()
    barrier = pltpu.get_barrier_semaphore()
    for offset in range(1, n):
        pl.semaphore_signal(
            barrier, inc=1, device_id={"chol": lax.rem(me + offset, n)}, device_id_type=MESH
        )
    pl.semaphore_signal(barrier, inc=1, device_id={"pop": 1 - pop}, device_id_type=MESH)
    gpad[pop * (walkers + 1)] = jnp.zeros((rows, basis), jnp.bfloat16)
    loads[0].wait()
    gpad[pl.ds(1, walkers)] = jnp.swapaxes(green[...].astype(jnp.float32), 0, 1).astype(jnp.bfloat16)
    loads[1].wait()
    dturn[...] = jnp.swapaxes(delta[...].astype(jnp.float32), 0, 1)
    pl.semaphore_wait(barrier, n)

    edge_green = pltpu.make_async_remote_copy(
        src_ref=gpad.at[1 + (1 - pop) * (walkers - 1)],
        dst_ref=gpad.at[pop * (walkers + 1)],
        send_sem=edge_send.at[0],
        recv_sem=edge_recv.at[0],
        device_id={"pop": 1 - pop},
        device_id_type=MESH,
    )
    edge_green_arrival = pltpu.make_async_remote_copy(
        src_ref=gpad.at[1 + (1 - pop) * (walkers - 1)],
        dst_ref=gpad.at[(1 - pop) * (walkers + 1)],
        send_sem=edge_send.at[0],
        recv_sem=edge_recv.at[0],
        device_id={"pop": 1 - pop},
        device_id_type=MESH,
    )
    edge_green.start()

    for ch in range(chunks):
        if ch == 1:
            edge_green_arrival.wait_recv()
        w0 = first_walker(jnp.int32(ch))
        for j in range(CHUNK):
            child = pop * walkers + w0 + j
            parent = parents[child]
            row = dturn[w0 + j]
            for k in range(3):
                chosen = jnp.where(parent == child - 1 + k, 1.0, 0.0)
                row = row + chosen * gpad[w0 + j + k].astype(jnp.float32)
            gall[w0 + j, orbital_rows(me), :] = row.astype(jnp.bfloat16)
        for chain in range(2):
            gather(jnp.int32(ch), chain, 0).start()

    for step in range(1, hops[0]):

        def forward(ch, carry, step=step):
            for chain in range(2):
                if step < hops[chain]:
                    gather_arrival(ch, chain, step - 1).wait_recv()
                    gather(ch, chain, step).start()
            return carry

        lax.fori_loop(0, chunks, forward, 0)

    loads[2].wait()
    row_ids = lax.broadcasted_iota(jnp.int32, (orbitals, 2 * orbitals), 0)
    col_ids = lax.broadcasted_iota(jnp.int32, (orbitals, 2 * orbitals), 1)
    diagonal = (row_ids == col_ids) | (row_ids + orbitals == col_ids)
    walker_ids = lax.broadcasted_iota(jnp.int32, (walkers, orbitals), 0)

    def add_and_forward(ch, step):
        for chain in range(2):
            if step < hops[chain]:
                scatter(ch, chain, step - 1).wait_recv()
                start_scatter(ch, chain, step)

    def compute(ch, total):
        for chain in range(2):
            gather_arrival(ch, chain, hops[chain] - 1).wait_recv()
        w0 = first_walker(ch)
        children = gall[pl.ds(w0, CHUNK)].reshape(CHUNK * orbitals, basis)
        turned = lax.dot_general(
            chol[...].reshape(vectors * orbitals, basis),
            children,
            (((1,), (1,)), ((), ())),
            preferred_element_type=jnp.float32,
        )
        low = turned.astype(jnp.bfloat16)
        rest = (turned - low.astype(jnp.float32)).astype(jnp.bfloat16)
        for j in range(CHUNK):
            mine = slice(j * orbitals, (j + 1) * orbitals)
            for g in range(vectors):
                cross[mine, g * orbitals : (g + 1) * orbitals] = low[
                    g * orbitals : (g + 1) * orbitals, mine
                ]
            products = jnp.dot(
                cross[mine, :],
                jnp.concatenate([low[:, mine], rest[:, mine]], axis=1),
                preferred_element_type=jnp.float32,
            )
            line = jnp.sum(jnp.where(diagonal, products, 0.0), axis=0, keepdims=True)
            line = line[:, :orbitals] + line[:, orbitals:]
            total = total + jnp.where(walker_ids == w0 + j, line, 0.0)
        force[pl.ds(w0, CHUNK)] = jnp.dot(
            cross[...],
            chol[...].reshape(vectors * orbitals, basis),
            preferred_element_type=jnp.float32,
        ).reshape(CHUNK, orbitals, basis)
        for chain in range(2):
            start_scatter(ch, chain, 0)

        @pl.when(ch > 0)
        def _():
            add_and_forward(ch - 1, 1)

        return total

    traces[me] = lax.fori_loop(0, chunks, compute, jnp.zeros((walkers, orbitals), jnp.float32))
    for offset in range(1, n):
        trace_copy(offset - 1, me, lax.rem(me + offset, n)).start()

    add_and_forward(jnp.int32(chunks - 1), 1)
    for step in range(2, hops[0]):

        def one_chunk(ch, carry, step=step):
            add_and_forward(ch, step)
            return carry

        lax.fori_loop(0, chunks, one_chunk, 0)

    edge_force = pltpu.make_async_remote_copy(
        src_ref=edge.at[0],
        dst_ref=edge.at[1],
        send_sem=edge_send.at[1],
        recv_sem=edge_recv.at[1],
        device_id={"pop": 1 - pop},
        device_id_type=MESH,
    )
    final[pop * (walkers + 1)] = jnp.zeros((rows, basis), jnp.float32)
    for ch in range(chunks):
        at = jnp.int32(ch)
        w0 = first_walker(at)
        for chain in range(2):
            scatter(at, chain, hops[chain] - 1).wait_recv()
        for j in range(CHUNK):
            final[w0 + j + 1] = scale * (
                force[w0 + j, orbital_rows(me), :]
                + arrived[0, hops[0] - 1, ch, j].astype(jnp.float32)
                + arrived[1, hops[1] - 1, ch, j].astype(jnp.float32)
            )
        if ch == 1:
            edge[0] = final[1 + (1 - pop) * (walkers - 1)].astype(jnp.bfloat16)
            edge_force.start()

    edge_force.wait_recv()
    final[(1 - pop) * (walkers + 1)] = edge[1].astype(jnp.float32)
    for w in range(walkers):
        parent = pop * walkers + w
        row = jnp.zeros((rows, basis), jnp.float32)
        for k in range(3):
            child = parent - 1 + k
            inside = (child >= 0) & (child < 2 * walkers)
            taken = parents[jnp.minimum(jnp.maximum(child, 0), 2 * walkers - 1)] == parent
            row = row + jnp.where(inside & taken, 1.0, 0.0) * final[w + k]
        copies = jnp.maximum(counts[w], 1).astype(jnp.float32)
        out[w] = (row / jnp.full((rows, basis), copies)).astype(jnp.bfloat16)

    for offset in range(1, n):
        trace_copy(offset - 1, lax.rem(me + n - offset, n), me).wait_recv()
    energy = traces[0]
    for i in range(1, n):
        energy = energy + traces[i]
    energy_out[...] = energy

    edge_green.wait_send()
    edge_force.wait_send()
    for offset in range(1, n):
        trace_copy(offset - 1, me, lax.rem(me + offset, n)).wait_send()

    def drain(ch, carry):
        for chain in range(2):
            for step in range(hops[chain]):
                gather(ch, chain, step).wait_send()
                scatter(ch, chain, step).wait_send()
        return carry

    lax.fori_loop(0, chunks, drain, 0)


def ring_shards(green_half, step_delta, chol_vectors, copy_counts, parents):
    n = lax.axis_size("chol")
    rows, walkers, basis = green_half.shape
    vectors, orbitals, _ = chol_vectors.shape
    hbm = pl.BlockSpec(memory_space=pltpu.HBM)
    chunks = walkers // CHUNK
    hops = n // 2
    smem = pl.BlockSpec(memory_space=pltpu.SMEM)
    vmem = pl.BlockSpec(memory_space=pltpu.VMEM)
    dma = pltpu.SemaphoreType.DMA
    wide = vectors * orbitals
    out, traces = pl.pallas_call(
        functools.partial(step_kernel, n),
        out_shape=(
            jax.ShapeDtypeStruct((walkers, rows, basis), jnp.bfloat16),
            jax.ShapeDtypeStruct((walkers, orbitals), jnp.float32),
        ),
        in_specs=[smem, smem, hbm, hbm, hbm],
        out_specs=(vmem, vmem),
        scratch_shapes=[
            pltpu.VMEM(green_half.shape, jnp.bfloat16),
            pltpu.VMEM(green_half.shape, jnp.bfloat16),
            pltpu.VMEM(chol_vectors.shape, jnp.bfloat16),
            pltpu.VMEM((walkers + 2, rows, basis), jnp.bfloat16),
            pltpu.VMEM((walkers, rows, basis), jnp.float32),
            pltpu.VMEM((walkers, orbitals, basis), jnp.bfloat16),
            pltpu.VMEM((CHUNK * orbitals, wide), jnp.bfloat16),
            pltpu.VMEM((walkers, orbitals, basis), jnp.float32),
            pltpu.VMEM((walkers, orbitals, basis), jnp.bfloat16),
            pltpu.VMEM((2, hops, chunks, CHUNK, rows, basis), jnp.bfloat16),
            pltpu.VMEM((walkers + 2, rows, basis), jnp.float32),
            pltpu.VMEM((2, rows, basis), jnp.bfloat16),
            pltpu.VMEM((n, walkers, orbitals), jnp.float32),
            dma((2, hops, chunks)),
            dma((2, hops, chunks)),
            dma((2, hops, chunks)),
            dma((2, hops, chunks)),
            dma((n - 1,)),
            dma((n - 1,)),
            dma((2,)),
            dma((2,)),
            dma((3,)),
        ],
        compiler_params=pltpu.CompilerParams(
            collective_id=0, has_side_effects=True, vmem_limit_bytes=63 * 1024 * 1024
        ),
        cost_estimate=pl.CostEstimate(
            flops=4 * walkers * orbitals * wide * basis,
            bytes_accessed=4 * walkers * orbitals * basis,
            transcendentals=0,
        ),
    )(
        parents,
        copy_counts,
        green_half,
        step_delta,
        chol_vectors,
    )
    energy = jnp.sum(traces, axis=1) * (-0.125 / (n * vectors * orbitals))
    return jnp.swapaxes(out, 0, 1), energy


def any_shards(green_half, step_delta, chol_vectors, copy_counts, parents):
    rows, walkers, basis = green_half.shape
    orbitals = chol_vectors.shape[1]
    n = lax.axis_size("chol")
    fits = (
        rows % 16 == 0
        and orbitals % 128 == 0
        and basis % 128 == 0
        and walkers == 4 * CHUNK
        and n % 2 == 0
        and n >= 4
        and lax.axis_size("pop") == 2
    )
    run = ring_shards if fits else shards
    return run(green_half, step_delta, chol_vectors, copy_counts, parents)


def solution(mesh):
    placed = (
        P(("rep", "chol"), "pop", None),
        P(("rep", "chol"), "pop", None),
        P(("rep", "chol"), None, None),
        P(("rep", "pop")),
        P("rep"),
    )
    return jax.shard_map(
        any_shards,
        mesh=mesh,
        in_specs=placed,
        out_specs=(P(("rep", "chol"), "pop", None), P(("rep", "pop"))),
        check_vma=False,
    )
```

```python
import functools

import jax
import jax.numpy as jnp
from jax import lax
from jax.experimental import pallas as pl
from jax.experimental.pallas import tpu as pltpu
from jax.sharding import PartitionSpec as P

MESH = pl.DeviceIdType.MESH
CHUNK = 2


def child_forces(child_rows, chol_vectors):
    total_chol = lax.axis_size("chol") * chol_vectors.shape[0]
    orbitals = chol_vectors.shape[1]
    factor = -1.0 / total_chol**0.5
    cross = jnp.einsum(
        "iwm,gkm->wgik",
        lax.all_gather(child_rows, "chol", axis=0, tiled=True),
        chol_vectors,
        preferred_element_type=jnp.float32,
    )
    cross_low = cross.astype(jnp.bfloat16)
    trace_part = jnp.sum(cross_low.astype(jnp.float32) * jnp.swapaxes(cross, 2, 3), axis=(1, 2, 3))
    energies = lax.psum(trace_part, "chol") * (-0.125 / (total_chol * orbitals))
    forces = lax.psum_scatter(
        factor
        * jnp.einsum("wgik,gil->kwl", cross_low, chol_vectors, preferred_element_type=jnp.float32),
        "chol",
        scatter_dimension=0,
        tiled=True,
    )
    return (forces, energies)


def shards(green_half, step_delta, chol_vectors, copy_counts, parents):
    per_group = green_half.shape[1]
    my_group = lax.axis_index("pop")
    all_parents = lax.all_gather(green_half, "pop", axis=1, tiled=True)
    my_parents = lax.dynamic_slice_in_dim(parents, my_group * per_group, per_group, 0)
    picked = jnp.take(all_parents, my_parents, axis=1)
    child_rows = (picked.astype(jnp.float32) + step_delta.astype(jnp.float32)).astype(jnp.bfloat16)
    forces, child_energy = child_forces(child_rows, chol_vectors)
    parent_slots = jnp.arange(all_parents.shape[1], dtype=jnp.int32)
    one_hot = (my_parents[:, None] == parent_slots[None, :]).astype(jnp.float32)
    spread_sum = jnp.einsum("kcl,cp->kpl", forces, one_hot, precision=lax.Precision.HIGHEST)
    summed = lax.psum_scatter(
        spread_sum.astype(jnp.bfloat16), "pop", scatter_dimension=1, tiled=True
    ).astype(jnp.float32)
    divisor = jnp.maximum(copy_counts, 1).astype(jnp.float32)
    parent_force = (summed / divisor[None, :, None]).astype(jnp.bfloat16)
    return (parent_force, child_energy)


def ring_device(pos, n):
    half = n // 2
    pos = lax.rem(pos + 2 * n, n)
    side = lax.div(pos, half)
    rest = lax.rem(pos, half)
    return 2 * ((1 - side) * rest + side * (half - 1 - rest)) + side


def step_kernel(
    n, parents, counts, green_in, delta_in, chol_in, out, energy_out,
    green, delta, chol, gpad, dturn, gall, cross, force, fsend, arrived, final, edge, traces,
    ag_send, ag_recv, rs_send, rs_recv, tr_send, tr_recv, edge_send, edge_recv, load_sem,
):
    rows, walkers, basis = green.shape
    vectors, orbitals, _ = chol.shape
    chunks = walkers // CHUNK
    me = lax.axis_index("chol")
    pop = lax.axis_index("pop")
    side = lax.rem(me, 2)
    level = lax.div(me, 2)
    pos = side * (n - 1 - level) + (1 - side) * level
    hops = (n // 2, n - 1 - n // 2)
    scale = -1.0 / (n * vectors) ** 0.5

    def first_walker(ch):
        late = jnp.minimum(lax.div(ch, 2), 1)
        k = late * ch + (1 - late) * (1 - ch)
        return CHUNK * (pop * k + (1 - pop) * (chunks - 1 - k))

    def sign(ch, chain):
        up = 1 - 2 * lax.rem(ch, 2)
        return up if chain == 0 else -up

    def orbital_rows(device):
        return pl.ds(pl.multiple_of(device * rows, rows), rows)

    def gather(ch, chain, step):
        way = sign(ch, chain)
        where = (pl.ds(first_walker(ch), CHUNK), orbital_rows(ring_device(pos - way * step, n)))
        return pltpu.make_async_remote_copy(
            src_ref=gall.at[where],
            dst_ref=gall.at[where],
            send_sem=ag_send.at[chain, step, ch],
            recv_sem=ag_recv.at[chain, step, ch],
            device_id={"chol": ring_device(pos + way, n)},
            device_id_type=MESH,
        )

    def gather_arrival(ch, chain, step):
        way = sign(ch, chain)
        where = (pl.ds(first_walker(ch), CHUNK), orbital_rows(ring_device(pos - way * (step + 1), n)))
        return pltpu.make_async_remote_copy(
            src_ref=gall.at[where],
            dst_ref=gall.at[where],
            send_sem=ag_send.at[chain, step, ch],
            recv_sem=ag_recv.at[chain, step, ch],
            device_id={"chol": ring_device(pos + way, n)},
            device_id_type=MESH,
        )

    def scatter(ch, chain, step):
        way = sign(ch, chain)
        target = orbital_rows(ring_device(pos + way * (hops[chain] - step), n))
        return pltpu.make_async_remote_copy(
            src_ref=fsend.at[pl.ds(first_walker(ch), CHUNK), target],
            dst_ref=arrived.at[chain, step, ch],
            send_sem=rs_send.at[chain, step, ch],
            recv_sem=rs_recv.at[chain, step, ch],
            device_id={"chol": ring_device(pos + way, n)},
            device_id_type=MESH,
        )

    def start_scatter(ch, chain, step):
        way = sign(ch, chain)
        target = orbital_rows(ring_device(pos + way * (hops[chain] - step), n))
        w0 = first_walker(ch)
        for j in range(CHUNK):
            part = force[w0 + j, target, :]
            if step > 0:
                part = part + arrived[chain, step - 1, ch, j].astype(jnp.float32)
            fsend[w0 + j, target, :] = part.astype(jnp.bfloat16)
        scatter(ch, chain, step).start()

    def trace_copy(offset, owner, peer):
        return pltpu.make_async_remote_copy(
            src_ref=traces.at[owner],
            dst_ref=traces.at[owner],
            send_sem=tr_send.at[offset],
            recv_sem=tr_recv.at[offset],
            device_id={"chol": peer},
            device_id_type=MESH,
        )

    loads = [
        pltpu.make_async_copy(green_in, green, load_sem.at[0]),
        pltpu.make_async_copy(delta_in, delta, load_sem.at[1]),
        pltpu.make_async_copy(chol_in, chol, load_sem.at[2]),
    ]
    for load in loads:
        load.start()
    barrier = pltpu.get_barrier_semaphore()
    for offset in range(1, n):
        pl.semaphore_signal(
            barrier, inc=1, device_id={"chol": lax.rem(me + offset, n)}, device_id_type=MESH
        )
    pl.semaphore_signal(barrier, inc=1, device_id={"pop": 1 - pop}, device_id_type=MESH)
    gpad[pop * (walkers + 1)] = jnp.zeros((rows, basis), jnp.bfloat16)
    loads[0].wait()
    gpad[pl.ds(1, walkers)] = jnp.swapaxes(green[...].astype(jnp.float32), 0, 1).astype(jnp.bfloat16)
    loads[1].wait()
    dturn[...] = jnp.swapaxes(delta[...].astype(jnp.float32), 0, 1)
    pl.semaphore_wait(barrier, n)

    edge_green = pltpu.make_async_remote_copy(
        src_ref=gpad.at[1 + (1 - pop) * (walkers - 1)],
        dst_ref=gpad.at[pop * (walkers + 1)],
        send_sem=edge_send.at[0],
        recv_sem=edge_recv.at[0],
        device_id={"pop": 1 - pop},
        device_id_type=MESH,
    )
    edge_green_arrival = pltpu.make_async_remote_copy(
        src_ref=gpad.at[1 + (1 - pop) * (walkers - 1)],
        dst_ref=gpad.at[(1 - pop) * (walkers + 1)],
        send_sem=edge_send.at[0],
        recv_sem=edge_recv.at[0],
        device_id={"pop": 1 - pop},
        device_id_type=MESH,
    )
    edge_green.start()

    def make_children(ch):
        w0 = first_walker(ch)
        for j in range(CHUNK):
            child = pop * walkers + w0 + j
            parent = parents[child]
            row = dturn[w0 + j]
            for k in range(3):
                chosen = jnp.where(parent == child - 1 + k, 1.0, 0.0)
                row = row + chosen * gpad[w0 + j + k].astype(jnp.float32)
            gall[w0 + j, orbital_rows(me), :] = row.astype(jnp.bfloat16)
        for chain in range(2):
            gather(ch, chain, 0).start()

    def forward(ch, step):
        for chain in range(2):
            if step < hops[chain]:
                gather_arrival(ch, chain, step - 1).wait_recv()
                gather(ch, chain, step).start()

    loads[2].wait()
    row_ids = lax.broadcasted_iota(jnp.int32, (orbitals, 2 * orbitals), 0)
    col_ids = lax.broadcasted_iota(jnp.int32, (orbitals, 2 * orbitals), 1)
    diagonal = (row_ids == col_ids) | (row_ids + orbitals == col_ids)
    walker_ids = lax.broadcasted_iota(jnp.int32, (walkers, orbitals), 0)

    def add_and_forward(ch, step):
        for chain in range(2):
            if step < hops[chain]:
                scatter(ch, chain, step - 1).wait_recv()
                start_scatter(ch, chain, step)

    def compute(ch):
        for chain in range(2):
            gather_arrival(ch, chain, hops[chain] - 1).wait_recv()
        w0 = first_walker(ch)
        children = gall[pl.ds(w0, CHUNK)].reshape(CHUNK * orbitals, basis)
        turned = lax.dot_general(
            chol[...].reshape(vectors * orbitals, basis),
            children,
            (((1,), (1,)), ((), ())),
            preferred_element_type=jnp.float32,
        )
        low = turned.astype(jnp.bfloat16)
        rest = (turned - low.astype(jnp.float32)).astype(jnp.bfloat16)
        for j in range(CHUNK):
            mine = slice(j * orbitals, (j + 1) * orbitals)
            for g in range(vectors):
                cross[mine, g * orbitals : (g + 1) * orbitals] = low[
                    g * orbitals : (g + 1) * orbitals, mine
                ]
            products = jnp.dot(
                cross[mine, :],
                jnp.concatenate([low[:, mine], rest[:, mine]], axis=1),
                preferred_element_type=jnp.float32,
            )
            line = jnp.sum(jnp.where(diagonal, products, 0.0), axis=0, keepdims=True)
            line = line[:, :orbitals] + line[:, orbitals:]
            traces[me] = traces[me] + jnp.where(walker_ids == w0 + j, line, 0.0)
        force[pl.ds(w0, CHUNK)] = jnp.dot(
            cross[...],
            chol[...].reshape(vectors * orbitals, basis),
            preferred_element_type=jnp.float32,
        ).reshape(CHUNK, orbitals, basis)
        for chain in range(2):
            start_scatter(ch, chain, 0)

    traces[me] = jnp.zeros((walkers, orbitals), jnp.float32)
    last = hops[0]
    delay = last - 1
    half = chunks // 2
    order = [last] + list(range(last)) + list(range(last + 1, 2 * last))

    def tick(now, carry):
        for stage in order:

            @pl.when((now == stage) | (now == stage + delay))
            def _(stage=stage):
                base = half * lax.div(now - stage, delay)

                def one_chunk(c, inner):
                    ch = base + c
                    if stage == 0:

                        @pl.when(ch == 1)
                        def _():
                            edge_green_arrival.wait_recv()

                        make_children(ch)
                    elif stage < last:
                        forward(ch, stage)
                    elif stage == last:
                        compute(ch)
                    else:
                        add_and_forward(ch, stage - last)
                    return inner

                lax.fori_loop(0, half, one_chunk, 0)

        return carry

    lax.fori_loop(0, last + delay + 1, tick, 0)
    for offset in range(1, n):
        trace_copy(offset - 1, me, lax.rem(me + offset, n)).start()

    def late_tick(now, carry):
        for stage in range(last + 1, 2 * last):

            @pl.when((now == stage) | (now == stage + delay))
            def _(stage=stage):
                base = half * lax.div(now - stage, delay)

                def one_chunk(c, inner):
                    add_and_forward(base + c, stage - last)
                    return inner

                lax.fori_loop(0, half, one_chunk, 0)

        return carry

    lax.fori_loop(last + delay + 1, 2 * last + delay, late_tick, 0)

    edge_force = pltpu.make_async_remote_copy(
        src_ref=edge.at[0],
        dst_ref=edge.at[1],
        send_sem=edge_send.at[1],
        recv_sem=edge_recv.at[1],
        device_id={"pop": 1 - pop},
        device_id_type=MESH,
    )
    final[pop * (walkers + 1)] = jnp.zeros((rows, basis), jnp.float32)

    def parent_row(order_index):
        w = pop * order_index + (1 - pop) * (walkers - 1 - order_index)
        parent = pop * walkers + w
        row = jnp.zeros((rows, basis), jnp.float32)
        for k in range(3):
            child = parent - 1 + k
            inside = (child >= 0) & (child < 2 * walkers)
            taken = parents[jnp.minimum(jnp.maximum(child, 0), 2 * walkers - 1)] == parent
            row = row + jnp.where(inside & taken, 1.0, 0.0) * final[w + k]
        copies = jnp.maximum(counts[w], 1).astype(jnp.float32)
        out[w] = (row / jnp.full((rows, basis), copies)).astype(jnp.bfloat16)

    early = walkers - CHUNK - 1
    for ch in range(chunks):
        at = jnp.int32(ch)
        w0 = first_walker(at)
        if ch == chunks - 1:
            edge_force.wait_recv()
            final[(1 - pop) * (walkers + 1)] = edge[1].astype(jnp.float32)
            for i in range(early):
                parent_row(i)
            for offset in range(1, n):
                trace_copy(offset - 1, lax.rem(me + n - offset, n), me).wait_recv()
            energy = traces[0]
            for i in range(1, n):
                energy = energy + traces[i]
            energy = jnp.sum(energy, axis=1, keepdims=True) * (-0.125 / (n * vectors * orbitals))
            energy_out[...] = jnp.broadcast_to(energy, energy_out.shape)
            edge_green.wait_send()
            edge_force.wait_send()
            for offset in range(1, n):
                trace_copy(offset - 1, me, lax.rem(me + offset, n)).wait_send()

            def drain(c, carry):
                for chain in range(2):
                    for step in range(hops[chain]):
                        gather(c, chain, step).wait_send()
                return carry

            lax.fori_loop(0, chunks, drain, 0)
        for chain in range(2):
            scatter(at, chain, hops[chain] - 1).wait_recv()
        for j in range(CHUNK):
            final[w0 + j + 1] = scale * (
                force[w0 + j, orbital_rows(me), :]
                + arrived[0, hops[0] - 1, ch, j].astype(jnp.float32)
                + arrived[1, hops[1] - 1, ch, j].astype(jnp.float32)
            )
        if ch == 1:
            edge[0] = final[1 + (1 - pop) * (walkers - 1)].astype(jnp.bfloat16)
            edge_force.start()

    for i in range(early, walkers):
        parent_row(i)

    def drain_sums(c, carry):
        for chain in range(2):
            for step in range(hops[chain]):
                scatter(c, chain, step).wait_send()
        return carry

    lax.fori_loop(0, chunks, drain_sums, 0)


def ring_shards(green_half, step_delta, chol_vectors, copy_counts, parents):
    n = lax.axis_size("chol")
    rows, walkers, basis = green_half.shape
    vectors, orbitals, _ = chol_vectors.shape
    hbm = pl.BlockSpec(memory_space=pltpu.HBM)
    chunks = walkers // CHUNK
    hops = n // 2
    smem = pl.BlockSpec(memory_space=pltpu.SMEM)
    vmem = pl.BlockSpec(memory_space=pltpu.VMEM)
    dma = pltpu.SemaphoreType.DMA
    wide = vectors * orbitals
    out, traces = pl.pallas_call(
        functools.partial(step_kernel, n),
        out_shape=(
            jax.ShapeDtypeStruct((walkers, rows, basis), jnp.bfloat16),
            jax.ShapeDtypeStruct((walkers, orbitals), jnp.float32),
        ),
        in_specs=[smem, smem, hbm, hbm, hbm],
        out_specs=(vmem, vmem),
        scratch_shapes=[
            pltpu.VMEM(green_half.shape, jnp.bfloat16),
            pltpu.VMEM(green_half.shape, jnp.bfloat16),
            pltpu.VMEM(chol_vectors.shape, jnp.bfloat16),
            pltpu.VMEM((walkers + 2, rows, basis), jnp.bfloat16),
            pltpu.VMEM((walkers, rows, basis), jnp.float32),
            pltpu.VMEM((walkers, orbitals, basis), jnp.bfloat16),
            pltpu.VMEM((CHUNK * orbitals, wide), jnp.bfloat16),
            pltpu.VMEM((walkers, orbitals, basis), jnp.float32),
            pltpu.VMEM((walkers, orbitals, basis), jnp.bfloat16),
            pltpu.VMEM((2, hops, chunks, CHUNK, rows, basis), jnp.bfloat16),
            pltpu.VMEM((walkers + 2, rows, basis), jnp.float32),
            pltpu.VMEM((2, rows, basis), jnp.bfloat16),
            pltpu.VMEM((n, walkers, orbitals), jnp.float32),
            dma((2, hops, chunks)),
            dma((2, hops, chunks)),
            dma((2, hops, chunks)),
            dma((2, hops, chunks)),
            dma((n - 1,)),
            dma((n - 1,)),
            dma((2,)),
            dma((2,)),
            dma((3,)),
        ],
        compiler_params=pltpu.CompilerParams(
            collective_id=0, has_side_effects=True, vmem_limit_bytes=62 * 1024 * 1024
        ),
        cost_estimate=pl.CostEstimate(
            flops=4 * walkers * orbitals * wide * basis,
            bytes_accessed=4 * walkers * orbitals * basis,
            transcendentals=0,
        ),
    )(
        parents,
        copy_counts,
        green_half,
        step_delta,
        chol_vectors,
    )
    return jnp.swapaxes(out, 0, 1), traces[:, 0]


def any_shards(green_half, step_delta, chol_vectors, copy_counts, parents):
    rows, walkers, basis = green_half.shape
    orbitals = chol_vectors.shape[1]
    n = lax.axis_size("chol")
    fits = (
        rows % 16 == 0
        and orbitals % 128 == 0
        and basis % 128 == 0
        and walkers == 4 * CHUNK
        and n % 2 == 0
        and n >= 4
        and lax.axis_size("pop") == 2
    )
    run = ring_shards if fits else shards
    return run(green_half, step_delta, chol_vectors, copy_counts, parents)


def solution(mesh):
    placed = (
        P(("rep", "chol"), "pop", None),
        P(("rep", "chol"), "pop", None),
        P(("rep", "chol"), None, None),
        P(("rep", "pop")),
        P("rep"),
    )
    return jax.shard_map(
        any_shards,
        mesh=mesh,
        in_specs=placed,
        out_specs=(P(("rep", "chol"), "pop", None), P(("rep", "pop"))),
        check_vma=False,
    )
```

```python
import functools

import jax
import jax.numpy as jnp
from jax import lax
from jax.experimental import pallas as pl
from jax.experimental.pallas import tpu as pltpu
from jax.sharding import PartitionSpec as P

MESH = pl.DeviceIdType.MESH
CHUNK = 2


def child_forces(child_rows, chol_vectors):
    total_chol = lax.axis_size("chol") * chol_vectors.shape[0]
    orbitals = chol_vectors.shape[1]
    factor = -1.0 / total_chol**0.5
    cross = jnp.einsum(
        "iwm,gkm->wgik",
        lax.all_gather(child_rows, "chol", axis=0, tiled=True),
        chol_vectors,
        preferred_element_type=jnp.float32,
    )
    cross_low = cross.astype(jnp.bfloat16)
    trace_part = jnp.sum(cross_low.astype(jnp.float32) * jnp.swapaxes(cross, 2, 3), axis=(1, 2, 3))
    energies = lax.psum(trace_part, "chol") * (-0.125 / (total_chol * orbitals))
    forces = lax.psum_scatter(
        factor
        * jnp.einsum("wgik,gil->kwl", cross_low, chol_vectors, preferred_element_type=jnp.float32),
        "chol",
        scatter_dimension=0,
        tiled=True,
    )
    return (forces, energies)


def shards(green_half, step_delta, chol_vectors, copy_counts, parents):
    per_group = green_half.shape[1]
    my_group = lax.axis_index("pop")
    all_parents = lax.all_gather(green_half, "pop", axis=1, tiled=True)
    my_parents = lax.dynamic_slice_in_dim(parents, my_group * per_group, per_group, 0)
    picked = jnp.take(all_parents, my_parents, axis=1)
    child_rows = (picked.astype(jnp.float32) + step_delta.astype(jnp.float32)).astype(jnp.bfloat16)
    forces, child_energy = child_forces(child_rows, chol_vectors)
    parent_slots = jnp.arange(all_parents.shape[1], dtype=jnp.int32)
    one_hot = (my_parents[:, None] == parent_slots[None, :]).astype(jnp.float32)
    spread_sum = jnp.einsum("kcl,cp->kpl", forces, one_hot, precision=lax.Precision.HIGHEST)
    summed = lax.psum_scatter(
        spread_sum.astype(jnp.bfloat16), "pop", scatter_dimension=1, tiled=True
    ).astype(jnp.float32)
    divisor = jnp.maximum(copy_counts, 1).astype(jnp.float32)
    parent_force = (summed / divisor[None, :, None]).astype(jnp.bfloat16)
    return (parent_force, child_energy)


def ring_device(pos, n):
    half = n // 2
    pos = lax.rem(pos + 2 * n, n)
    side = lax.div(pos, half)
    rest = lax.rem(pos, half)
    return 2 * ((1 - side) * rest + side * (half - 1 - rest)) + side


def step_kernel(
    n, parents, counts, green_in, delta_in, chol_in, out, energy_out,
    green, delta, chol, gpad, dturn, gall, cross, force, fsend, arrived, final, edge, traces,
    ag_send, ag_recv, rs_send, rs_recv, tr_send, tr_recv, edge_send, edge_recv, load_sem,
):
    rows, walkers, basis = green.shape
    vectors, orbitals, _ = chol.shape
    chunks = walkers // CHUNK
    me = lax.axis_index("chol")
    pop = lax.axis_index("pop")
    side = lax.rem(me, 2)
    level = lax.div(me, 2)
    pos = side * (n - 1 - level) + (1 - side) * level
    hops = (n // 2, n - 1 - n // 2)
    scale = -1.0 / (n * vectors) ** 0.5

    def first_walker(ch):
        late = jnp.minimum(lax.div(ch, 2), 1)
        k = late * ch + (1 - late) * (1 - ch)
        return CHUNK * (pop * k + (1 - pop) * (chunks - 1 - k))

    def sign(ch, chain):
        up = 1 - 2 * lax.rem(ch, 2)
        return up if chain == 0 else -up

    def orbital_rows(device):
        return pl.ds(pl.multiple_of(device * rows, rows), rows)

    def gather(ch, chain, step):
        way = sign(ch, chain)
        where = (pl.ds(first_walker(ch), CHUNK), orbital_rows(ring_device(pos - way * step, n)))
        return pltpu.make_async_remote_copy(
            src_ref=gall.at[where],
            dst_ref=gall.at[where],
            send_sem=ag_send.at[chain, step, ch],
            recv_sem=ag_recv.at[chain, step, ch],
            device_id={"chol": ring_device(pos + way, n)},
            device_id_type=MESH,
        )

    def gather_arrival(ch, chain, step):
        way = sign(ch, chain)
        where = (pl.ds(first_walker(ch), CHUNK), orbital_rows(ring_device(pos - way * (step + 1), n)))
        return pltpu.make_async_remote_copy(
            src_ref=gall.at[where],
            dst_ref=gall.at[where],
            send_sem=ag_send.at[chain, step, ch],
            recv_sem=ag_recv.at[chain, step, ch],
            device_id={"chol": ring_device(pos + way, n)},
            device_id_type=MESH,
        )

    def scatter(ch, chain, step):
        way = sign(ch, chain)
        target = orbital_rows(ring_device(pos + way * (hops[chain] - step), n))
        return pltpu.make_async_remote_copy(
            src_ref=fsend.at[pl.ds(first_walker(ch), CHUNK), target],
            dst_ref=arrived.at[chain, step, ch],
            send_sem=rs_send.at[chain, step, ch],
            recv_sem=rs_recv.at[chain, step, ch],
            device_id={"chol": ring_device(pos + way, n)},
            device_id_type=MESH,
        )

    def start_scatter(ch, chain, step):
        way = sign(ch, chain)
        target = orbital_rows(ring_device(pos + way * (hops[chain] - step), n))
        w0 = first_walker(ch)
        for j in range(CHUNK):
            part = force[w0 + j, target, :]
            if step > 0:
                part = part + arrived[chain, step - 1, ch, j].astype(jnp.float32)
            fsend[w0 + j, target, :] = part.astype(jnp.bfloat16)
        scatter(ch, chain, step).start()

    def trace_copy(offset, owner, peer):
        return pltpu.make_async_remote_copy(
            src_ref=traces.at[owner],
            dst_ref=traces.at[owner],
            send_sem=tr_send.at[offset],
            recv_sem=tr_recv.at[offset],
            device_id={"chol": peer},
            device_id_type=MESH,
        )

    loads = [
        pltpu.make_async_copy(green_in, green, load_sem.at[0]),
        pltpu.make_async_copy(delta_in, delta, load_sem.at[1]),
        pltpu.make_async_copy(chol_in, chol, load_sem.at[2]),
    ]
    for load in loads:
        load.start()
    barrier = pltpu.get_barrier_semaphore()
    for offset in range(1, n):
        pl.semaphore_signal(
            barrier, inc=1, device_id={"chol": lax.rem(me + offset, n)}, device_id_type=MESH
        )
    pl.semaphore_signal(barrier, inc=1, device_id={"pop": 1 - pop}, device_id_type=MESH)
    gpad[pop * (walkers + 1)] = jnp.zeros((rows, basis), jnp.bfloat16)
    loads[0].wait()
    gpad[pl.ds(1, walkers)] = jnp.swapaxes(green[...].astype(jnp.float32), 0, 1).astype(jnp.bfloat16)
    loads[1].wait()
    dturn[...] = jnp.swapaxes(delta[...].astype(jnp.float32), 0, 1)
    pl.semaphore_wait(barrier, n)

    edge_green = pltpu.make_async_remote_copy(
        src_ref=gpad.at[1 + (1 - pop) * (walkers - 1)],
        dst_ref=gpad.at[pop * (walkers + 1)],
        send_sem=edge_send.at[0],
        recv_sem=edge_recv.at[0],
        device_id={"pop": 1 - pop},
        device_id_type=MESH,
    )
    edge_green_arrival = pltpu.make_async_remote_copy(
        src_ref=gpad.at[1 + (1 - pop) * (walkers - 1)],
        dst_ref=gpad.at[(1 - pop) * (walkers + 1)],
        send_sem=edge_send.at[0],
        recv_sem=edge_recv.at[0],
        device_id={"pop": 1 - pop},
        device_id_type=MESH,
    )
    edge_green.start()

    def make_children(ch):
        w0 = first_walker(ch)
        for j in range(CHUNK):
            child = pop * walkers + w0 + j
            parent = parents[child]
            row = dturn[w0 + j]
            for k in range(3):
                chosen = jnp.where(parent == child - 1 + k, 1.0, 0.0)
                row = row + chosen * gpad[w0 + j + k].astype(jnp.float32)
            gall[w0 + j, orbital_rows(me), :] = row.astype(jnp.bfloat16)
        for chain in range(2):
            gather(ch, chain, 0).start()

    def forward(ch, step):
        for chain in range(2):
            if step < hops[chain]:
                gather_arrival(ch, chain, step - 1).wait_recv()
                gather(ch, chain, step).start()

    loads[2].wait()
    row_ids = lax.broadcasted_iota(jnp.int32, (orbitals, 2 * orbitals), 0)
    col_ids = lax.broadcasted_iota(jnp.int32, (orbitals, 2 * orbitals), 1)
    diagonal = (row_ids == col_ids) | (row_ids + orbitals == col_ids)
    walker_ids = lax.broadcasted_iota(jnp.int32, (walkers, orbitals), 0)

    def add_and_forward(ch, step):
        for chain in range(2):
            if step < hops[chain]:
                scatter(ch, chain, step - 1).wait_recv()
                start_scatter(ch, chain, step)

    def compute(ch):
        for chain in range(2):
            gather_arrival(ch, chain, hops[chain] - 1).wait_recv()
        w0 = first_walker(ch)
        children = gall[pl.ds(w0, CHUNK)].reshape(CHUNK * orbitals, basis)
        turned = lax.dot_general(
            chol[...].reshape(vectors * orbitals, basis),
            children,
            (((1,), (1,)), ((), ())),
            preferred_element_type=jnp.float32,
        )
        low = turned.astype(jnp.bfloat16)
        rest = (turned - low.astype(jnp.float32)).astype(jnp.bfloat16)
        for j in range(CHUNK):
            mine = slice(j * orbitals, (j + 1) * orbitals)
            for g in range(vectors):
                cross[mine, g * orbitals : (g + 1) * orbitals] = low[
                    g * orbitals : (g + 1) * orbitals, mine
                ]
            products = jnp.dot(
                cross[mine, :],
                jnp.concatenate([low[:, mine], rest[:, mine]], axis=1),
                preferred_element_type=jnp.float32,
            )
            line = jnp.sum(jnp.where(diagonal, products, 0.0), axis=0, keepdims=True)
            line = line[:, :orbitals] + line[:, orbitals:]
            traces[me] = traces[me] + jnp.where(walker_ids == w0 + j, line, 0.0)
        force[pl.ds(w0, CHUNK)] = jnp.dot(
            cross[...],
            chol[...].reshape(vectors * orbitals, basis),
            preferred_element_type=jnp.float32,
        ).reshape(CHUNK, orbitals, basis)
        for chain in range(2):
            start_scatter(ch, chain, 0)

    traces[me] = jnp.zeros((walkers, orbitals), jnp.float32)
    last = hops[0]

    def per_chunk(act):
        def body(ch, carry):
            act(ch)
            return carry

        lax.fori_loop(0, chunks, body, 0)

    def begin(ch):
        @pl.when(ch == 1)
        def _():
            edge_green_arrival.wait_recv()

        make_children(ch)

    def compute_and_sum(ch):
        compute(ch)

        @pl.when(ch > 0)
        def _():
            add_and_forward(ch - 1, 1)

    per_chunk(begin)
    for step in range(1, last):
        per_chunk(functools.partial(forward, step=step))
    per_chunk(compute_and_sum)
    for offset in range(1, n):
        trace_copy(offset - 1, me, lax.rem(me + offset, n)).start()
    add_and_forward(jnp.int32(chunks - 1), 1)
    for step in range(2, last):
        per_chunk(functools.partial(add_and_forward, step=step))

    edge_force = pltpu.make_async_remote_copy(
        src_ref=edge.at[0],
        dst_ref=edge.at[1],
        send_sem=edge_send.at[1],
        recv_sem=edge_recv.at[1],
        device_id={"pop": 1 - pop},
        device_id_type=MESH,
    )
    final[pop * (walkers + 1)] = jnp.zeros((rows, basis), jnp.float32)

    def parent_row(order_index):
        w = pop * order_index + (1 - pop) * (walkers - 1 - order_index)
        parent = pop * walkers + w
        row = jnp.zeros((rows, basis), jnp.float32)
        for k in range(3):
            child = parent - 1 + k
            inside = (child >= 0) & (child < 2 * walkers)
            taken = parents[jnp.minimum(jnp.maximum(child, 0), 2 * walkers - 1)] == parent
            row = row + jnp.where(inside & taken, 1.0, 0.0) * final[w + k]
        copies = jnp.maximum(counts[w], 1).astype(jnp.float32)
        out[w] = (row / jnp.full((rows, basis), copies)).astype(jnp.bfloat16)

    early = walkers - CHUNK - 1
    for ch in range(chunks):
        at = jnp.int32(ch)
        w0 = first_walker(at)
        if ch == chunks - 1:
            edge_force.wait_recv()
            final[(1 - pop) * (walkers + 1)] = edge[1].astype(jnp.float32)
            for i in range(early):
                parent_row(i)
            for offset in range(1, n):
                trace_copy(offset - 1, lax.rem(me + n - offset, n), me).wait_recv()
            energy = traces[0]
            for i in range(1, n):
                energy = energy + traces[i]
            energy = jnp.sum(energy, axis=1, keepdims=True) * (-0.125 / (n * vectors * orbitals))
            energy_out[...] = jnp.broadcast_to(energy, energy_out.shape)
            edge_green.wait_send()
            edge_force.wait_send()
            for offset in range(1, n):
                trace_copy(offset - 1, me, lax.rem(me + offset, n)).wait_send()

            def drain(c, carry):
                for chain in range(2):
                    for step in range(hops[chain]):
                        gather(c, chain, step).wait_send()
                return carry

            lax.fori_loop(0, chunks, drain, 0)
        for chain in range(2):
            scatter(at, chain, hops[chain] - 1).wait_recv()
        for j in range(CHUNK):
            final[w0 + j + 1] = scale * (
                force[w0 + j, orbital_rows(me), :]
                + arrived[0, hops[0] - 1, ch, j].astype(jnp.float32)
                + arrived[1, hops[1] - 1, ch, j].astype(jnp.float32)
            )
        if ch == 1:
            edge[0] = final[1 + (1 - pop) * (walkers - 1)].astype(jnp.bfloat16)
            edge_force.start()

    for i in range(early, walkers):
        parent_row(i)

    def drain_sums(c, carry):
        for chain in range(2):
            for step in range(hops[chain]):
                scatter(c, chain, step).wait_send()
        return carry

    lax.fori_loop(0, chunks, drain_sums, 0)


def ring_shards(green_half, step_delta, chol_vectors, copy_counts, parents):
    n = lax.axis_size("chol")
    rows, walkers, basis = green_half.shape
    vectors, orbitals, _ = chol_vectors.shape
    hbm = pl.BlockSpec(memory_space=pltpu.HBM)
    chunks = walkers // CHUNK
    hops = n // 2
    smem = pl.BlockSpec(memory_space=pltpu.SMEM)
    vmem = pl.BlockSpec(memory_space=pltpu.VMEM)
    dma = pltpu.SemaphoreType.DMA
    wide = vectors * orbitals
    out, traces = pl.pallas_call(
        functools.partial(step_kernel, n),
        out_shape=(
            jax.ShapeDtypeStruct((walkers, rows, basis), jnp.bfloat16),
            jax.ShapeDtypeStruct((walkers, orbitals), jnp.float32),
        ),
        in_specs=[smem, smem, hbm, hbm, hbm],
        out_specs=(vmem, vmem),
        scratch_shapes=[
            pltpu.VMEM(green_half.shape, jnp.bfloat16),
            pltpu.VMEM(green_half.shape, jnp.bfloat16),
            pltpu.VMEM(chol_vectors.shape, jnp.bfloat16),
            pltpu.VMEM((walkers + 2, rows, basis), jnp.bfloat16),
            pltpu.VMEM((walkers, rows, basis), jnp.float32),
            pltpu.VMEM((walkers, orbitals, basis), jnp.bfloat16),
            pltpu.VMEM((CHUNK * orbitals, wide), jnp.bfloat16),
            pltpu.VMEM((walkers, orbitals, basis), jnp.float32),
            pltpu.VMEM((walkers, orbitals, basis), jnp.bfloat16),
            pltpu.VMEM((2, hops, chunks, CHUNK, rows, basis), jnp.bfloat16),
            pltpu.VMEM((walkers + 2, rows, basis), jnp.float32),
            pltpu.VMEM((2, rows, basis), jnp.bfloat16),
            pltpu.VMEM((n, walkers, orbitals), jnp.float32),
            dma((2, hops, chunks)),
            dma((2, hops, chunks)),
            dma((2, hops, chunks)),
            dma((2, hops, chunks)),
            dma((n - 1,)),
            dma((n - 1,)),
            dma((2,)),
            dma((2,)),
            dma((3,)),
        ],
        compiler_params=pltpu.CompilerParams(
            collective_id=0, has_side_effects=True, vmem_limit_bytes=63 * 1024 * 1024
        ),
        cost_estimate=pl.CostEstimate(
            flops=4 * walkers * orbitals * wide * basis,
            bytes_accessed=4 * walkers * orbitals * basis,
            transcendentals=0,
        ),
    )(
        parents,
        copy_counts,
        green_half,
        step_delta,
        chol_vectors,
    )
    return jnp.swapaxes(out, 0, 1), traces[:, 0]


def any_shards(green_half, step_delta, chol_vectors, copy_counts, parents):
    rows, walkers, basis = green_half.shape
    orbitals = chol_vectors.shape[1]
    n = lax.axis_size("chol")
    fits = (
        rows % 16 == 0
        and orbitals % 128 == 0
        and basis % 128 == 0
        and walkers == 4 * CHUNK
        and n % 2 == 0
        and n >= 4
        and lax.axis_size("pop") == 2
    )
    run = ring_shards if fits else shards
    return run(green_half, step_delta, chol_vectors, copy_counts, parents)


def solution(mesh):
    placed = (
        P(("rep", "chol"), "pop", None),
        P(("rep", "chol"), "pop", None),
        P(("rep", "chol"), None, None),
        P(("rep", "pop")),
        P("rep"),
    )
    return jax.shard_map(
        any_shards,
        mesh=mesh,
        in_specs=placed,
        out_specs=(P(("rep", "chol"), "pop", None), P(("rep", "pop"))),
        check_vma=False,
    )
```
